32 devices in a mesh: harm: 4 (over y, x), node: 8 (over z, core).
Axes of the slice: x: 2, y: 2, z: 4, core: 2. Of those that a mesh axis runs over, the one named last changes fastest.
Arguments:
- voltages: float32 [128, 8192], P('harm', 'node'), may hold values from -6 to 6
- conductance: float32 [64, 3, 128, 128], P('node'), may hold values from -0.3125 to 0.3125
- capacitance: float32 [64, 3, 128, 128], P('node'), may hold values from -0.3125 to 0.3125
- pattern: int32 [64, 3], P('node'), may hold values from 0 to 63, as said below
- samples: float32 [256, 8192], P(None, 'node'), may hold values from 0.1 to 2
- terminals: int32 [2, 8192], P(None, 'node'), may hold values from 0 to 8191, as said below
Outputs:
- product: float32 [128, 8192], P('harm', 'node')
The draws below stay inside these ranges and needn't reach their ends.
Inputs may be any that keep to these rules, and one draw needn't show every extreme that they name: `pattern`: slot 0 of row block r is r itself; every slot names a block within one block of the 8 row blocks of the device that holds r; the first row block of every device but the first names the block just before that range in slot 1, the last row block of every device but the last names the block just after it in slot 2. `terminals`: branch m belongs to the device holding nodes from 1024 * (m // 1024) on; its first terminal lies among that device's 1024 nodes, its second among those or the 128 nodes after them.
All inputs are finite; a program needn't handle non-finite values.
Results may differ from the reference program's by a relative error of at most 0.0003.
Values sent between devices are 32-bit elements; how exact they have to be, the bound alone decides.
A program may use at most 64 MiB of HBM per device.

```python
import math
import jax
import jax.numpy as jnp
from jax import lax

C = 128
S = 256
BLK = 128
KB = 3
NB = 8
MB = 1024
ND = 1024
NODES = 8192
NBT = 64
MT = 8192


def draw_pattern(key, part):
    row_index = jnp.arange(NBT, dtype=jnp.int32)
    owner_dev = row_index // NB
    low_end = jnp.maximum(owner_dev * NB - 1, 0)
    high_end = jnp.minimum(owner_dev * NB + NB + 1, NBT)
    chosen = jax.random.randint(key, (NBT, KB - 1), low_end[:, None], high_end[:, None], dtype=jnp.int32)
    first_row = (row_index % NB == 0) & (owner_dev > 0)
    last_row = (row_index % NB == NB - 1) & (owner_dev < NBT // NB - 1)
    chosen = chosen.at[:, 0].set(jnp.where(first_row, owner_dev * NB - 1, chosen[:, 0]))
    chosen = chosen.at[:, 1].set(jnp.where(last_row, owner_dev * NB + NB, chosen[:, 1]))
    return jnp.concatenate([row_index[:, None], chosen], axis=1)


def draw_terminals(key, part):
    branch_index = jnp.arange(MT, dtype=jnp.int32)
    holder = branch_index // MB
    start_node = holder * ND
    first_key, second_key = jax.random.split(key)
    first_end = jax.random.randint(first_key, (MT,), start_node, start_node + ND, dtype=jnp.int32)
    second_end = jax.random.randint(second_key, (MT,), start_node, jnp.minimum(start_node + ND + BLK, NODES), dtype=jnp.int32)
    return jnp.stack([first_end, second_end], axis=0)


def block_levels(stream_key, extent, cuts, smallest, high):
    def one(position, blocks):
        draws = jax.random.uniform(jax.random.fold_in(jax.random.fold_in(stream_key, 6), position), (blocks,), jnp.float32, smallest / len(cuts), high / len(cuts))
        return jnp.repeat(jnp.exp(draws), extent[position] // blocks).reshape((-1,) + (1,) * (len(extent) - position - 1))

    loudness = one(*cuts[0])
    for cut in cuts[1:]:
        loudness = loudness * one(*cut)
    return loudness


def noise(stream_key, shape, width, bound, cuts=(), held_as=jnp.bfloat16):
    result = width * jax.random.normal(stream_key, shape, jnp.float32)
    if cuts:
        result = result * block_levels(stream_key, shape, cuts, -0.22, 0.18)
    return jnp.clip(result, -bound, bound).astype(held_as)


def setup_inputs(seed: int = 0) -> dict:
    keys = jax.random.split(jax.random.key(seed), 7)
    voltages = noise(keys[0], (C, NODES), 1.0, 6.0, ((0, 4), (1, 8)), jnp.float32)
    conductance = noise(keys[1], (NBT, KB, BLK, BLK), (KB * BLK) ** -0.5, 0.3125, ((0, 8),), jnp.float32)
    capacitance = noise(keys[2], (NBT, KB, BLK, BLK), (KB * BLK) ** -0.5, 0.3125, ((0, 8),), jnp.float32)
    pattern = draw_pattern(jax.random.fold_in(keys[6], 71), 0)
    samples = jnp.clip(jnp.exp(math.log(2.0) - 2.9957323 * jax.random.uniform(keys[4], (S, MT), jnp.float32) ** block_levels(keys[4], (S, MT), ((1, 8),), -0.2, 0.2)), 0.1, 2.0)
    terminals = draw_terminals(jax.random.fold_in(keys[6], 71), 0)
    return dict(voltages=voltages, conductance=conductance, capacitance=capacitance, pattern=pattern, samples=samples, terminals=terminals)


highest = lax.Precision.HIGHEST


def transform_tables(column_count, period):
    harmonic = jnp.arange(column_count // 2, dtype=jnp.int32)
    sample_index = jnp.arange(period, dtype=jnp.int32)
    phases = (sample_index[:, None] * harmonic[None, :]) % period
    angles = phases.astype(jnp.float32) * (2.0 * math.pi / period)
    forward = jnp.stack([jnp.cos(angles), -jnp.sin(angles)], axis=2).reshape(period, column_count)
    backward = forward.T * (2.0 / period)
    return forward, backward


def rotate_pairs(field, angular):
    column_count, width_now = field.shape
    paired = field.reshape(column_count // 2, 2, width_now)
    turned = jnp.stack([-paired[:, 1], paired[:, 0]], axis=1) * angular[:, None, None]
    return turned.reshape(column_count, width_now)


def reference(voltages, conductance, capacitance, pattern, samples, terminals):
    column_count, node_count = voltages.shape
    node_tiles = voltages.reshape(column_count, node_count // BLK, BLK)

    def row_block(inputs):
        columns, g_tile, c_tile = inputs
        picked = jnp.take(node_tiles, columns.astype(jnp.int32), axis=1)
        g_part = jnp.einsum("cjk,jkl->cl", picked, g_tile, precision=highest)
        c_part = jnp.einsum("cjk,jkl->cl", picked, c_tile, precision=highest)
        return g_part, c_part

    g_rows, c_rows = lax.map(row_block, (pattern, conductance, capacitance))
    conductive = g_rows.transpose(1, 0, 2).reshape(column_count, node_count)
    capacitive = c_rows.transpose(1, 0, 2).reshape(column_count, node_count)
    angular = jnp.arange(column_count // 2, dtype=jnp.float32) / (column_count // 2)
    linear = conductive + rotate_pairs(capacitive, angular)
    first_end = terminals[0].astype(jnp.int32)
    second_end = terminals[1].astype(jnp.int32)
    branch = jnp.take(voltages, first_end, axis=1) - jnp.take(voltages, second_end, axis=1)
    forward, backward = transform_tables(column_count, samples.shape[0])
    wave = jnp.dot(forward, branch, precision=highest) * samples
    current = jnp.dot(backward, wave, precision=highest)
    injected = jnp.zeros_like(voltages).at[:, first_end].add(current).at[:, second_end].add(-current)
    return linear + injected
```

```python
import functools
import math

import jax
import jax.numpy as jnp
import ml_dtypes
import numpy as np
from jax import lax
from jax.experimental import pallas as pl
from jax.experimental.pallas import tpu as pltpu
from jax.sharding import PartitionSpec as P

MESH = pl.DeviceIdType.MESH
f32, bf16 = jnp.float32, jnp.bfloat16


def halves(value):
    high = value.astype(bf16).astype(f32)
    return jnp.concatenate([high, value - high], axis=0).astype(bf16)


def dot(a, b):
    return jnp.dot(a, b, preferred_element_type=f32)


def dot_t(a, b):
    return lax.dot_general(a, b, (((1,), (1,)), ((), ())), preferred_element_type=f32)


def kernel(
    H, N, parts, dup,
    pat, term, v_in, g_in, c_in, s_in, f_in, b_in,
    out,
    v_vm, g_vm, c_vm, s_vm, f_vm, b_vm,
    vext, halo, ends, send_b, recv_b, send_c, recv_c, send_s, recv_s, lin,
    load_sem, gc_sem,
    low_send, low_recv, halo_send, halo_recv,
    b_send, b_recv, c_send, c_recv, s_send, s_recv,
):
    h, n = lax.axis_index("harm"), lax.axis_index("node")
    rows, nodes = v_vm.shape
    blocks, slots, blk, _ = g_vm.shape
    chunk = s_vm.shape[1]
    part, twin = h // dup, lax.rem(h, dup)
    offset = pl.multiple_of(part * chunk, 128)

    load_v = pltpu.make_async_copy(v_in, v_vm, load_sem.at[0])
    load_f = pltpu.make_async_copy(f_in, f_vm, load_sem.at[1])
    load_b = pltpu.make_async_copy(b_in, b_vm, load_sem.at[2])
    load_s = pltpu.make_async_copy(s_in.at[:, pl.ds(offset, chunk)], s_vm, load_sem.at[3])
    loads = [load_v, load_f, load_b, load_s]
    half = blocks // 2
    gc_loads = []
    for k in range(2):
        rng = pl.ds(k * half, half)
        gc_loads.append(pltpu.make_async_copy(g_in.at[rng], g_vm.at[rng], gc_sem.at[2 * k]))
        gc_loads.append(pltpu.make_async_copy(c_in.at[rng], c_vm.at[rng], gc_sem.at[2 * k + 1]))
    for load in loads + gc_loads:
        load.start()

    barrier = pltpu.get_barrier_semaphore()

    def greet(to_h, to_n):
        pl.semaphore_signal(barrier, inc=1, device_id=(to_h, to_n), device_id_type=MESH)

    for d in range(1, H):
        greet(lax.rem(h + d, H), n)

    @pl.when(n > 0)
    def _():
        for d in range(H):
            greet(lax.rem(h + d, H), n - 1)

    @pl.when(n < N - 1)
    def _():
        for d in range(H):
            greet(lax.rem(h + d, H), n + 1)

    def greeted():
        sides = jnp.where(n > 0, H, 0) + jnp.where(n < N - 1, H, 0)
        pl.semaphore_wait(barrier, H - 1 + sides)

    def remote(src, dst, send, recv, to_h, to_n):
        return pltpu.make_async_remote_copy(
            src_ref=src, dst_ref=dst, send_sem=send, recv_sem=recv,
            device_id=(to_h, to_n), device_id_type=MESH,
        )

    to_high = remote(
        vext.at[blocks], vext.at[0], low_send.at[0], low_recv.at[0], h, lax.rem(n + 1, N)
    )
    to_low = [
        remote(
            vext.at[1], halo.at[h], halo_send.at[d], halo_recv.at[d],
            lax.rem(h + d, H), lax.rem(n + N - 1, N),
        )
        for d in range(H)
    ]
    spills = []
    for i in range(parts):
        to_h = lax.rem(part + i, parts) * dup + twin
        spills.append(
            remote(send_s.at[to_h], recv_s.at[i], s_send.at[i], s_recv.at[i], to_h, lax.rem(n + 1, N))
        )

    load_v.wait()
    for b in range(blocks):
        vext[b + 1] = v_vm[:, b * blk : (b + 1) * blk]
    stacked = halves(v_vm[...])

    to_parts = []
    step = min(256, nodes)
    for i in [*range(1, parts), 0]:
        q = lax.rem(part + i, parts)
        at = pl.multiple_of(q * chunk, 128)
        first = term[0:1, pl.ds(at, chunk)] - n * nodes
        second = term[1:2, pl.ds(at, chunk)] - n * nodes
        first = jnp.where(first == second, -1, first)
        second = jnp.where(first == -1, -1, second)
        piece = jnp.zeros((2 * rows, chunk), f32)
        for k in range(0, nodes, step):
            row = lax.broadcasted_iota(jnp.int32, (step, chunk), 0) + k
            hot = jnp.where(row == first, 1.0, jnp.where(row == second, -1.0, 0.0)).astype(bf16)
            ends[q, k : k + step, :] = hot
            piece += dot(stacked[:, k : k + step], hot)
        piece = piece[:rows] + piece[rows:]
        if i == 0:
            recv_b[h] = piece
        if i or dup > 1:
            send_b[q] = piece
        if i == (1 if parts > 1 else 0):
            greeted()

            @pl.when(n > 0)
            def _():
                for copy in to_low:
                    copy.start()

            @pl.when(n < N - 1)
            def _():
                to_high.start()

        for j in range(dup):
            if i or j:
                to_h = q * dup + lax.rem(twin + j, dup)
                e = i * dup + j
                copy = remote(send_b.at[q], recv_b.at[h], b_send.at[e], b_recv.at[e], to_h, n)
                copy.start()
                to_parts.append(copy)

    @pl.when(n > 0)
    def _():
        to_high.wait_recv()

    @pl.when(n == 0)
    def _():
        vext[0] = jnp.zeros((rows, blk), f32)
        recv_s[...] = jnp.zeros(recv_s.shape, f32)

    @pl.when(n < N - 1)
    def _():
        for copy in to_low:
            copy.wait_recv()

    @pl.when(n == N - 1)
    def _():
        halo[...] = jnp.zeros(halo.shape, f32)

    vext[blocks + 1] = halo[h]

    line = lax.broadcasted_iota(jnp.int32, (rows, blk), 0)
    harmonic = h * (rows // 2) + line // 2
    omega = harmonic.astype(f32) / (H * rows // 2)
    odd = lax.rem(line, 2) == 1

    def linear(r):
        at = [jnp.clip(pat[r, j] - (n * blocks - 1), 0, blocks + 1) for j in range(slots)]
        picks = [vext[at[j]] for j in range(slots)]
        picked = halves(jnp.concatenate(picks, axis=1))
        weight = jnp.concatenate(
            [g_vm[r].reshape(slots * blk, blk), c_vm[r].reshape(slots * blk, blk)], axis=1
        )
        high = weight.astype(bf16)
        low = (weight - high.astype(f32)).astype(bf16)
        main = dot(picked, high)
        rest = dot(picked, low)
        both = main[:rows] + (main[rows:] + rest[:rows])
        conductive, capacitive = both[:, :blk], both[:, blk:]
        turned = jnp.where(
            odd, pltpu.roll(capacitive, 1, 0), -pltpu.roll(capacitive, rows - 1, 0)
        )
        lin[:, r * blk : (r + 1) * blk] = conductive + omega * turned

    for load in gc_loads[:2]:
        load.wait()
    for r in range(half):
        linear(r)

    for copy in to_parts:
        copy.wait_recv()
    first = term[0:1, pl.ds(offset, chunk)] - n * nodes
    second = term[1:2, pl.ds(offset, chunk)] - n * nodes
    row = lax.broadcasted_iota(jnp.int32, (blk, chunk), 0) + nodes
    beyond = jnp.where(row == second, -1.0, 0.0).astype(bf16)
    columns = H * rows
    above = dot(halves(halo[...].reshape(columns, blk)), beyond)
    branch = recv_b[...].reshape(columns, chunk) + (above[:columns] + above[columns:])
    branch_high = branch.astype(bf16)
    branch_low = (branch - branch_high.astype(f32)).astype(bf16)
    load_f.wait()
    load_s.wait()
    wave = dot(f_vm[...], jnp.concatenate([branch_high, branch_low, branch_high], axis=0))
    wave = wave * s_vm[...]
    wave_high = wave.astype(bf16)
    wave_low = (wave - wave_high.astype(f32)).astype(bf16)
    load_b.wait()
    current = dot(b_vm[...], jnp.concatenate([wave_high, wave_low, wave_high], axis=0))
    send_c[...] = current.reshape(H, rows, chunk)
    recv_c[part] = send_c[h]
    to_harm = [None]
    for i in range(1, parts):
        to_h = lax.rem(part + i, parts) * dup + twin
        copy = remote(send_c.at[to_h], recv_c.at[part], c_send.at[i], c_recv.at[i], to_h, n)
        copy.start()
        to_harm.append(copy)
    spill = dot_t(halves(current), beyond)
    send_s[...] = (spill[:columns] + spill[columns:]).reshape(H, rows, blk)

    @pl.when(n < N - 1)
    def _():
        for copy in spills:
            copy.start()

    for load in gc_loads[2:]:
        load.wait()
    for r in range(half, blocks):
        linear(r)

    total = lin[...]
    for i in range(parts):
        q = lax.rem(part + parts - i, parts)
        if i:
            to_harm[i].wait_recv()
        added = dot_t(halves(recv_c[q]), ends[q])
        total = total + (added[:rows] + added[rows:])

    @pl.when(n > 0)
    def _():
        for copy in spills:
            copy.wait_recv()

    arrival = recv_s[0]
    for i in range(1, parts):
        arrival = arrival + recv_s[i]
    out[:, :blk] = total[:, :blk] + arrival
    out[:, blk:] = total[:, blk:]

    for copy in to_parts + to_harm[1:]:
        copy.wait_send()

    @pl.when(n > 0)
    def _():
        for copy in to_low:
            copy.wait_send()

    @pl.when(n < N - 1)
    def _():
        to_high.wait_send()
        for copy in spills:
            copy.wait_send()


def tables(columns, period):
    harmonic = np.arange(columns // 2)
    phases = (np.arange(period)[:, None] * harmonic[None, :]) % period
    angles = phases * (2.0 * math.pi / period)
    forward = np.stack([np.cos(angles), -np.sin(angles)], axis=2).reshape(period, columns)
    backward = forward.T * (2.0 / period)

    def three(table):
        high = table.astype(ml_dtypes.bfloat16)
        low = (table - high.astype(np.float64)).astype(ml_dtypes.bfloat16)
        return jnp.asarray(np.concatenate([high, high, low], axis=1))

    return three(forward), three(backward)


def per_device(voltages, conductance, capacitance, pattern, samples, terminals):
    rows, nodes = voltages.shape
    blocks, slots, blk, _ = conductance.shape
    period, branches = samples.shape
    H, N = lax.axis_size("harm"), lax.axis_size("node")
    parts = min(H, branches // 128)
    dup = H // parts
    chunk = branches // parts
    forward, backward = tables(H * rows, period)
    dma = pltpu.SemaphoreType.DMA
    anywhere = pl.BlockSpec(memory_space=pltpu.MemorySpace.HBM)
    return pl.pallas_call(
        functools.partial(kernel, H, N, parts, dup),
        out_shape=jax.ShapeDtypeStruct((rows, nodes), f32),
        in_specs=[
            pl.BlockSpec(memory_space=pltpu.MemorySpace.SMEM),
            pl.BlockSpec(memory_space=pltpu.MemorySpace.VMEM),
        ]
        + [anywhere] * 6,
        out_specs=pl.BlockSpec(memory_space=pltpu.MemorySpace.VMEM),
        scratch_shapes=[
            pltpu.VMEM((rows, nodes), f32),
            pltpu.VMEM(conductance.shape, f32),
            pltpu.VMEM(capacitance.shape, f32),
            pltpu.VMEM((period, chunk), f32),
            pltpu.VMEM(forward.shape, bf16),
            pltpu.VMEM(backward.shape, bf16),
            pltpu.VMEM((blocks + 2, rows, blk), f32),
            pltpu.VMEM((H, rows, blk), f32),
            pltpu.VMEM((parts, nodes, chunk), bf16),
            pltpu.VMEM((parts, rows, chunk), f32),
            pltpu.VMEM((H, rows, chunk), f32),
            pltpu.VMEM((H, rows, chunk), f32),
            pltpu.VMEM((parts, rows, chunk), f32),
            pltpu.VMEM((H, rows, blk), f32),
            pltpu.VMEM((parts, rows, blk), f32),
            pltpu.VMEM((rows, nodes), f32),
            dma((4,)),
            dma((4,)),
            dma((1,)),
            dma((1,)),
            dma((H,)),
            dma((H,)),
            dma((H,)),
            dma((H,)),
            dma((parts,)),
            dma((parts,)),
            dma((parts,)),
            dma((parts,)),
        ],
        compiler_params=pltpu.CompilerParams(
            collective_id=0, has_side_effects=True, vmem_limit_bytes=40 * 1024 * 1024
        ),
    )(pattern, terminals, voltages, conductance, capacitance, samples, forward, backward)


def solution(mesh):
    in_specs = (
        P("harm", "node"),
        P("node", None, None, None),
        P("node", None, None, None),
        P("node", None),
        P(None, "node"),
        P(None, "node"),
    )
    out_specs = P("harm", "node")
    return jax.shard_map(
        per_device, mesh=mesh, in_specs=in_specs, out_specs=out_specs, check_vma=False
    )
```

```python
import functools
import math

import jax
import jax.numpy as jnp
import ml_dtypes
import numpy as np
from jax import lax
from jax.experimental import pallas as pl
from jax.experimental.pallas import tpu as pltpu
from jax.sharding import PartitionSpec as P

MESH = pl.DeviceIdType.MESH
f32, bf16 = jnp.float32, jnp.bfloat16


def halves(value):
    high = value.astype(bf16).astype(f32)
    return jnp.concatenate([high, value - high], axis=0).astype(bf16)


def dot(a, b):
    return jnp.dot(a, b, preferred_element_type=f32)


def dot_t(a, b):
    return lax.dot_general(a, b, (((1,), (1,)), ((), ())), preferred_element_type=f32)


def kernel(
    H, N, parts, dup,
    pat, term, v_in, g_in, c_in, s_in, f_in, b_in,
    out,
    v_vm, g_vm, c_vm, s_vm, f_vm, b_vm,
    vext, halo, ends, send_b, recv_b, send_c, recv_c, send_s, recv_s, lin,
    load_sem, gc_sem,
    low_send, low_recv, halo_send, halo_recv,
    b_send, b_recv, c_send, c_recv, s_send, s_recv,
):
    h, n = lax.axis_index("harm"), lax.axis_index("node")
    rows, nodes = v_vm.shape
    blocks, slots, blk, _ = g_vm.shape
    chunk = s_vm.shape[1]
    part, twin = h // dup, lax.rem(h, dup)
    offset = pl.multiple_of(part * chunk, 128)

    load_v = pltpu.make_async_copy(v_in, v_vm, load_sem.at[0])
    load_f = pltpu.make_async_copy(f_in, f_vm, load_sem.at[1])
    load_b = pltpu.make_async_copy(b_in, b_vm, load_sem.at[2])
    load_s = pltpu.make_async_copy(s_in.at[:, pl.ds(offset, chunk)], s_vm, load_sem.at[3])
    loads = [load_v, load_f, load_b, load_s]
    half = blocks // 2
    gc_loads = []
    for k in range(2):
        rng = pl.ds(k * half, half)
        gc_loads.append(pltpu.make_async_copy(g_in.at[rng], g_vm.at[rng], gc_sem.at[2 * k]))
        gc_loads.append(pltpu.make_async_copy(c_in.at[rng], c_vm.at[rng], gc_sem.at[2 * k + 1]))
    for load in loads + gc_loads:
        load.start()

    barrier = pltpu.get_barrier_semaphore()

    def greet(to_h, to_n):
        pl.semaphore_signal(barrier, inc=1, device_id=(to_h, to_n), device_id_type=MESH)

    for d in range(1, H):
        greet(lax.rem(h + d, H), n)

    @pl.when(n > 0)
    def _():
        for d in range(H):
            greet(lax.rem(h + d, H), n - 1)

    @pl.when(n < N - 1)
    def _():
        for d in range(H):
            greet(lax.rem(h + d, H), n + 1)

    def greeted():
        sides = jnp.where(n > 0, H, 0) + jnp.where(n < N - 1, H, 0)
        pl.semaphore_wait(barrier, H - 1 + sides)

    def remote(src, dst, send, recv, to_h, to_n):
        return pltpu.make_async_remote_copy(
            src_ref=src, dst_ref=dst, send_sem=send, recv_sem=recv,
            device_id=(to_h, to_n), device_id_type=MESH,
        )

    to_high = remote(
        vext.at[blocks], vext.at[0], low_send.at[0], low_recv.at[0], h, lax.rem(n + 1, N)
    )
    to_low = [
        remote(
            vext.at[1], halo.at[h], halo_send.at[d], halo_recv.at[d],
            lax.rem(h + d, H), lax.rem(n + N - 1, N),
        )
        for d in range(H)
    ]
    spills = []
    for i in range(parts):
        to_h = lax.rem(part + i, parts) * dup + twin
        spills.append(
            remote(send_s.at[to_h], recv_s.at[i], s_send.at[i], s_recv.at[i], to_h, lax.rem(n + 1, N))
        )

    load_v.wait()
    for b in range(blocks):
        vext[b + 1] = v_vm[:, b * blk : (b + 1) * blk]
    stacked = halves(v_vm[...])

    to_parts = []
    step = min(256, nodes)
    for i in [*range(1, parts), 0]:
        q = lax.rem(part + i, parts)
        at = pl.multiple_of(q * chunk, 128)
        first = term[0:1, pl.ds(at, chunk)] - n * nodes
        second = term[1:2, pl.ds(at, chunk)] - n * nodes
        first = jnp.where(first == second, -1, first)
        second = jnp.where(first == -1, -1, second)
        piece = jnp.zeros((2 * rows, chunk), f32)
        for k in range(0, nodes, step):
            row = lax.broadcasted_iota(jnp.int32, (step, chunk), 0) + k
            hot = jnp.where(row == first, 1.0, jnp.where(row == second, -1.0, 0.0)).astype(bf16)
            ends[q, k : k + step, :] = hot
            piece += dot(stacked[:, k : k + step], hot)
        piece = piece[:rows] + piece[rows:]
        if i == 0:
            recv_b[h] = piece
        if i or dup > 1:
            send_b[q] = piece
        if i == (1 if parts > 1 else 0):
            greeted()

            @pl.when(n > 0)
            def _():
                for copy in to_low:
                    copy.start()

            @pl.when(n < N - 1)
            def _():
                to_high.start()

        for j in range(dup):
            if i or j:
                to_h = q * dup + lax.rem(twin + j, dup)
                e = i * dup + j
                copy = remote(send_b.at[q], recv_b.at[h], b_send.at[e], b_recv.at[e], to_h, n)
                copy.start()
                to_parts.append(copy)

    @pl.when(n > 0)
    def _():
        to_high.wait_recv()

    @pl.when(n == 0)
    def _():
        vext[0] = jnp.zeros((rows, blk), f32)
        recv_s[...] = jnp.zeros(recv_s.shape, f32)

    @pl.when(n < N - 1)
    def _():
        for copy in to_low:
            copy.wait_recv()

    @pl.when(n == N - 1)
    def _():
        halo[...] = jnp.zeros(halo.shape, f32)

    vext[blocks + 1] = halo[h]

    line = lax.broadcasted_iota(jnp.int32, (rows, blk), 0)
    harmonic = h * (rows // 2) + line // 2
    omega = harmonic.astype(f32) / (H * rows // 2)
    odd = lax.rem(line, 2) == 1

    def linear(r):
        at = [jnp.clip(pat[j, r] - (n * blocks - 1), 0, blocks + 1) for j in range(slots)]
        picks = [vext[at[j]] for j in range(slots)]
        picked = halves(jnp.concatenate(picks, axis=1))
        weight = jnp.concatenate(
            [g_vm[r].reshape(slots * blk, blk), c_vm[r].reshape(slots * blk, blk)], axis=1
        )
        high = weight.astype(bf16)
        low = (weight - high.astype(f32)).astype(bf16)
        main = dot(picked, high)
        rest = dot(picked, low)
        both = main[:rows] + (main[rows:] + rest[:rows])
        conductive, capacitive = both[:, :blk], both[:, blk:]
        turned = jnp.where(
            odd, pltpu.roll(capacitive, 1, 0), -pltpu.roll(capacitive, rows - 1, 0)
        )
        lin[:, r * blk : (r + 1) * blk] = conductive + omega * turned

    for load in gc_loads[:2]:
        load.wait()
    for r in range(half):
        linear(r)

    for copy in to_parts:
        copy.wait_recv()
    first = term[0:1, pl.ds(offset, chunk)] - n * nodes
    second = term[1:2, pl.ds(offset, chunk)] - n * nodes
    row = lax.broadcasted_iota(jnp.int32, (blk, chunk), 0) + nodes
    beyond = jnp.where(row == second, -1.0, 0.0).astype(bf16)
    columns = H * rows
    above = dot(halves(halo[...].reshape(columns, blk)), beyond)
    branch = recv_b[...].reshape(columns, chunk) + (above[:columns] + above[columns:])
    branch_high = branch.astype(bf16)
    branch_low = (branch - branch_high.astype(f32)).astype(bf16)
    load_f.wait()
    load_s.wait()
    wave = dot(f_vm[...], jnp.concatenate([branch_high, branch_low, branch_high], axis=0))
    wave = wave * s_vm[...]
    wave_high = wave.astype(bf16)
    wave_low = (wave - wave_high.astype(f32)).astype(bf16)
    load_b.wait()
    current = dot(b_vm[...], jnp.concatenate([wave_high, wave_low, wave_high], axis=0))
    send_c[...] = current.reshape(H, rows, chunk)
    recv_c[part] = send_c[h]
    to_harm = [None]
    for i in range(1, parts):
        to_h = lax.rem(part + i, parts) * dup + twin
        copy = remote(send_c.at[to_h], recv_c.at[part], c_send.at[i], c_recv.at[i], to_h, n)
        copy.start()
        to_harm.append(copy)
    spill = dot_t(halves(current), beyond)
    send_s[...] = (spill[:columns] + spill[columns:]).reshape(H, rows, blk)

    @pl.when(n < N - 1)
    def _():
        for copy in spills:
            copy.start()

    for load in gc_loads[2:]:
        load.wait()
    for r in range(half, blocks):
        linear(r)

    total = lin[...]
    for i in range(parts):
        q = lax.rem(part + parts - i, parts)
        if i:
            to_harm[i].wait_recv()
        added = dot_t(halves(recv_c[q]), ends[q])
        total = total + (added[:rows] + added[rows:])

    @pl.when(n > 0)
    def _():
        for copy in spills:
            copy.wait_recv()

    arrival = recv_s[0]
    for i in range(1, parts):
        arrival = arrival + recv_s[i]
    out[:, :blk] = total[:, :blk] + arrival
    out[:, blk:] = total[:, blk:]

    for copy in to_parts + to_harm[1:]:
        copy.wait_send()

    @pl.when(n > 0)
    def _():
        for copy in to_low:
            copy.wait_send()

    @pl.when(n < N - 1)
    def _():
        to_high.wait_send()
        for copy in spills:
            copy.wait_send()


def tables(columns, period):
    harmonic = np.arange(columns // 2)
    phases = (np.arange(period)[:, None] * harmonic[None, :]) % period
    angles = phases * (2.0 * math.pi / period)
    forward = np.stack([np.cos(angles), -np.sin(angles)], axis=2).reshape(period, columns)
    backward = forward.T * (2.0 / period)

    def three(table):
        high = table.astype(ml_dtypes.bfloat16)
        low = (table - high.astype(np.float64)).astype(ml_dtypes.bfloat16)
        return jnp.asarray(np.concatenate([high, high, low], axis=1))

    return three(forward), three(backward)


def per_device(voltages, conductance, capacitance, pattern, samples, terminals):
    rows, nodes = voltages.shape
    blocks, slots, blk, _ = conductance.shape
    period, branches = samples.shape
    H, N = lax.axis_size("harm"), lax.axis_size("node")
    parts = min(H, branches // 128)
    dup = H // parts
    chunk = branches // parts
    forward, backward = tables(H * rows, period)
    dma = pltpu.SemaphoreType.DMA
    anywhere = pl.BlockSpec(memory_space=pltpu.MemorySpace.HBM)
    return pl.pallas_call(
        functools.partial(kernel, H, N, parts, dup),
        out_shape=jax.ShapeDtypeStruct((rows, nodes), f32),
        in_specs=[
            pl.BlockSpec(memory_space=pltpu.MemorySpace.SMEM),
            pl.BlockSpec(memory_space=pltpu.MemorySpace.VMEM),
        ]
        + [anywhere] * 6,
        out_specs=pl.BlockSpec(memory_space=pltpu.MemorySpace.VMEM),
        scratch_shapes=[
            pltpu.VMEM((rows, nodes), f32),
            pltpu.VMEM(conductance.shape, f32),
            pltpu.VMEM(capacitance.shape, f32),
            pltpu.VMEM((period, chunk), f32),
            pltpu.VMEM(forward.shape, bf16),
            pltpu.VMEM(backward.shape, bf16),
            pltpu.VMEM((blocks + 2, rows, blk), f32),
            pltpu.VMEM((H, rows, blk), f32),
            pltpu.VMEM((parts, nodes, chunk), bf16),
            pltpu.VMEM((parts, rows, chunk), f32),
            pltpu.VMEM((H, rows, chunk), f32),
            pltpu.VMEM((H, rows, chunk), f32),
            pltpu.VMEM((parts, rows, chunk), f32),
            pltpu.VMEM((H, rows, blk), f32),
            pltpu.VMEM((parts, rows, blk), f32),
            pltpu.VMEM((rows, nodes), f32),
            dma((4,)),
            dma((4,)),
            dma((1,)),
            dma((1,)),
            dma((H,)),
            dma((H,)),
            dma((H,)),
            dma((H,)),
            dma((parts,)),
            dma((parts,)),
            dma((parts,)),
            dma((parts,)),
        ],
        compiler_params=pltpu.CompilerParams(
            collective_id=0, has_side_effects=True, vmem_limit_bytes=63 * 1024 * 1024
        ),
    )(pattern.T, terminals, voltages, conductance, capacitance, samples, forward, backward)


def solution(mesh):
    in_specs = (
        P("harm", "node"),
        P("node", None, None, None),
        P("node", None, None, None),
        P("node", None),
        P(None, "node"),
        P(None, "node"),
    )
    out_specs = P("harm", "node")
    return jax.shard_map(
        per_device, mesh=mesh, in_specs=in_specs, out_specs=out_specs, check_vma=False
    )
```

```python
import functools
import math

import jax
import jax.numpy as jnp
import ml_dtypes
import numpy as np
from jax import lax
from jax.experimental import pallas as pl
from jax.experimental.pallas import tpu as pltpu
from jax.sharding import PartitionSpec as P

MESH = pl.DeviceIdType.MESH
f32, bf16 = jnp.float32, jnp.bfloat16


def halves(value):
    high = value.astype(bf16).astype(f32)
    return jnp.concatenate([high, value - high], axis=0).astype(bf16)


def dot(a, b):
    return jnp.dot(a, b, preferred_element_type=f32)


def dot_t(a, b):
    return lax.dot_general(a, b, (((1,), (1,)), ((), ())), preferred_element_type=f32)


def kernel(
    H, N, parts, dup,
    pat_in, term_in, v_in, g_in, c_in, s_in, f_in, b_in,
    out,
    pat, term, v_vm, g_vm, c_vm, s_vm, f_vm, b_vm,
    vext, halo, ends, send_b, recv_b, send_c, recv_c, send_s, recv_s, lin,
    load_sem, gc_sem,
    low_send, low_recv, halo_send, halo_recv,
    b_send, b_recv, c_send, c_recv, s_send, s_recv,
):
    h, n = lax.axis_index("harm"), lax.axis_index("node")
    rows, nodes = v_vm.shape
    blocks, slots, blk, _ = g_vm.shape
    chunk = s_vm.shape[1]
    part, twin = h // dup, lax.rem(h, dup)
    offset = pl.multiple_of(part * chunk, 128)

    barrier = pltpu.get_barrier_semaphore()

    def greet(to_h, to_n):
        pl.semaphore_signal(barrier, inc=1, device_id=(to_h, to_n), device_id_type=MESH)

    for d in range(1, H):
        greet(lax.rem(h + d, H), n)

    @pl.when(n > 0)
    def _():
        for d in range(H):
            greet(lax.rem(h + d, H), n - 1)

    @pl.when(n < N - 1)
    def _():
        for d in range(H):
            greet(lax.rem(h + d, H), n + 1)

    load_v = pltpu.make_async_copy(v_in, v_vm, load_sem.at[0])
    load_f = pltpu.make_async_copy(f_in, f_vm, load_sem.at[1])
    load_b = pltpu.make_async_copy(b_in, b_vm, load_sem.at[2])
    load_s = pltpu.make_async_copy(s_in.at[:, pl.ds(offset, chunk)], s_vm, load_sem.at[3])
    load_t = pltpu.make_async_copy(term_in, term, load_sem.at[4])
    load_p = pltpu.make_async_copy(pat_in, pat, load_sem.at[5])
    loads = [load_v, load_t, load_p, load_f, load_b, load_s]
    half = blocks // 2
    gc_loads = []
    for k in range(2):
        rng = pl.ds(k * half, half)
        gc_loads.append(pltpu.make_async_copy(g_in.at[rng], g_vm.at[rng], gc_sem.at[2 * k]))
        gc_loads.append(pltpu.make_async_copy(c_in.at[rng], c_vm.at[rng], gc_sem.at[2 * k + 1]))
    for load in loads + gc_loads:
        load.start()

    def greeted():
        sides = jnp.where(n > 0, H, 0) + jnp.where(n < N - 1, H, 0)
        pl.semaphore_wait(barrier, H - 1 + sides)

    def remote(src, dst, send, recv, to_h, to_n):
        return pltpu.make_async_remote_copy(
            src_ref=src, dst_ref=dst, send_sem=send, recv_sem=recv,
            device_id=(to_h, to_n), device_id_type=MESH,
        )

    to_high = remote(
        vext.at[blocks], vext.at[0], low_send.at[0], low_recv.at[0], h, lax.rem(n + 1, N)
    )
    to_low = [
        remote(
            vext.at[1], halo.at[h], halo_send.at[d], halo_recv.at[d],
            lax.rem(h + d, H), lax.rem(n + N - 1, N),
        )
        for d in range(H)
    ]
    spills = []
    for i in range(parts):
        to_h = lax.rem(part + i, parts) * dup + twin
        spills.append(
            remote(send_s.at[to_h], recv_s.at[i], s_send.at[i], s_recv.at[i], to_h, lax.rem(n + 1, N))
        )

    load_t.wait()
    load_v.wait()
    for b in range(blocks):
        vext[b + 1] = v_vm[:, b * blk : (b + 1) * blk]
    stacked = halves(v_vm[...])

    to_parts = []
    step = min(256, nodes)
    for i in [*range(1, parts), 0]:
        q = lax.rem(part + i, parts)
        at = pl.multiple_of(q * chunk, 128)
        first = term[0:1, pl.ds(at, chunk)] - n * nodes
        second = term[1:2, pl.ds(at, chunk)] - n * nodes
        first = jnp.where(first == second, -1, first)
        second = jnp.where(first == -1, -1, second)
        piece = jnp.zeros((2 * rows, chunk), f32)
        for k in range(0, nodes, step):
            row = lax.broadcasted_iota(jnp.int32, (step, chunk), 0) + k
            hot = jnp.where(row == first, 1.0, jnp.where(row == second, -1.0, 0.0)).astype(bf16)
            ends[q, k : k + step, :] = hot
            piece += dot(stacked[:, k : k + step], hot)
        piece = piece[:rows] + piece[rows:]
        if i == 0:
            recv_b[h] = piece
        if i or dup > 1:
            send_b[q] = piece
        if i == (1 if parts > 1 else 0):
            greeted()

            @pl.when(n > 0)
            def _():
                for copy in to_low:
                    copy.start()

            @pl.when(n < N - 1)
            def _():
                to_high.start()

        for j in range(dup):
            if i or j:
                to_h = q * dup + lax.rem(twin + j, dup)
                e = i * dup + j
                copy = remote(send_b.at[q], recv_b.at[h], b_send.at[e], b_recv.at[e], to_h, n)
                copy.start()
                to_parts.append(copy)

    @pl.when(n > 0)
    def _():
        to_high.wait_recv()

    @pl.when(n == 0)
    def _():
        vext[0] = jnp.zeros((rows, blk), f32)
        recv_s[...] = jnp.zeros(recv_s.shape, f32)

    @pl.when(n < N - 1)
    def _():
        for copy in to_low:
            copy.wait_recv()

    @pl.when(n == N - 1)
    def _():
        halo[...] = jnp.zeros(halo.shape, f32)

    vext[blocks + 1] = halo[h]

    line = lax.broadcasted_iota(jnp.int32, (rows, blk), 0)
    harmonic = h * (rows // 2) + line // 2
    omega = harmonic.astype(f32) / (H * rows // 2)
    odd = lax.rem(line, 2) == 1

    def linear(r):
        at = [jnp.clip(pat[j, r] - (n * blocks - 1), 0, blocks + 1) for j in range(slots)]
        picks = [vext[at[j]] for j in range(slots)]
        picked = halves(jnp.concatenate(picks, axis=1))
        weight = jnp.concatenate(
            [g_vm[r].reshape(slots * blk, blk), c_vm[r].reshape(slots * blk, blk)], axis=1
        )
        high = weight.astype(bf16)
        low = (weight - high.astype(f32)).astype(bf16)
        main = dot(picked, high)
        rest = dot(picked, low)
        both = main[:rows] + (main[rows:] + rest[:rows])
        conductive, capacitive = both[:, :blk], both[:, blk:]
        turned = jnp.where(
            odd, pltpu.roll(capacitive, 1, 0), -pltpu.roll(capacitive, rows - 1, 0)
        )
        lin[:, r * blk : (r + 1) * blk] = conductive + omega * turned

    load_p.wait()
    for load in gc_loads[:2]:
        load.wait()
    for r in range(half):
        linear(r)

    for copy in to_parts:
        copy.wait_recv()
    first = term[0:1, pl.ds(offset, chunk)] - n * nodes
    second = term[1:2, pl.ds(offset, chunk)] - n * nodes
    row = lax.broadcasted_iota(jnp.int32, (blk, chunk), 0) + nodes
    beyond = jnp.where(row == second, -1.0, 0.0).astype(bf16)
    columns = H * rows
    above = dot(halves(halo[...].reshape(columns, blk)), beyond)
    branch = recv_b[...].reshape(columns, chunk) + (above[:columns] + above[columns:])
    branch_high = branch.astype(bf16)
    branch_low = (branch - branch_high.astype(f32)).astype(bf16)
    load_f.wait()
    load_s.wait()
    wave = dot(f_vm[...], jnp.concatenate([branch_high, branch_low, branch_high], axis=0))
    wave = wave * s_vm[...]
    wave_high = wave.astype(bf16)
    wave_low = (wave - wave_high.astype(f32)).astype(bf16)
    load_b.wait()
    current = dot(b_vm[...], jnp.concatenate([wave_high, wave_low, wave_high], axis=0))
    send_c[...] = current.reshape(H, rows, chunk)
    recv_c[part] = send_c[h]
    to_harm = [None]
    for i in range(1, parts):
        to_h = lax.rem(part + i, parts) * dup + twin
        copy = remote(send_c.at[to_h], recv_c.at[part], c_send.at[i], c_recv.at[i], to_h, n)
        copy.start()
        to_harm.append(copy)
    spill = dot_t(halves(current), beyond)
    send_s[...] = (spill[:columns] + spill[columns:]).reshape(H, rows, blk)

    @pl.when(n < N - 1)
    def _():
        for copy in spills:
            copy.start()

    for load in gc_loads[2:]:
        load.wait()
    for r in range(half, blocks):
        linear(r)

    total = lin[...]
    for i in range(parts):
        q = lax.rem(part + parts - i, parts)
        if i:
            to_harm[i].wait_recv()
        added = dot_t(halves(recv_c[q]), ends[q])
        total = total + (added[:rows] + added[rows:])

    @pl.when(n > 0)
    def _():
        for copy in spills:
            copy.wait_recv()

    arrival = recv_s[0]
    for i in range(1, parts):
        arrival = arrival + recv_s[i]
    out[:, :blk] = total[:, :blk] + arrival
    out[:, blk:] = total[:, blk:]

    for copy in to_parts + to_harm[1:]:
        copy.wait_send()

    @pl.when(n > 0)
    def _():
        for copy in to_low:
            copy.wait_send()

    @pl.when(n < N - 1)
    def _():
        to_high.wait_send()
        for copy in spills:
            copy.wait_send()


def tables(columns, period):
    harmonic = np.arange(columns // 2)
    phases = (np.arange(period)[:, None] * harmonic[None, :]) % period
    angles = phases * (2.0 * math.pi / period)
    forward = np.stack([np.cos(angles), -np.sin(angles)], axis=2).reshape(period, columns)
    backward = forward.T * (2.0 / period)

    def three(table):
        high = table.astype(ml_dtypes.bfloat16)
        low = (table - high.astype(np.float64)).astype(ml_dtypes.bfloat16)
        return jnp.asarray(np.concatenate([high, high, low], axis=1))

    return three(forward), three(backward)


def per_device(voltages, conductance, capacitance, pattern, samples, terminals):
    rows, nodes = voltages.shape
    blocks, slots, blk, _ = conductance.shape
    period, branches = samples.shape
    H, N = lax.axis_size("harm"), lax.axis_size("node")
    parts = min(H, branches // 128)
    dup = H // parts
    chunk = branches // parts
    forward, backward = tables(H * rows, period)
    dma = pltpu.SemaphoreType.DMA
    anywhere = pl.BlockSpec(memory_space=pltpu.MemorySpace.HBM)
    return pl.pallas_call(
        functools.partial(kernel, H, N, parts, dup),
        out_shape=pltpu.VMEM((rows, nodes), f32),
        in_specs=[anywhere] * 8,
        out_specs=pl.BlockSpec(memory_space=pltpu.MemorySpace.VMEM),
        scratch_shapes=[
            pltpu.SMEM(pattern.shape[::-1], jnp.int32),
            pltpu.VMEM(terminals.shape, jnp.int32),
            pltpu.VMEM((rows, nodes), f32),
            pltpu.VMEM(conductance.shape, f32),
            pltpu.VMEM(capacitance.shape, f32),
            pltpu.VMEM((period, chunk), f32),
            pltpu.VMEM(forward.shape, bf16),
            pltpu.VMEM(backward.shape, bf16),
            pltpu.VMEM((blocks + 2, rows, blk), f32),
            pltpu.VMEM((H, rows, blk), f32),
            pltpu.VMEM((parts, nodes, chunk), bf16),
            pltpu.VMEM((parts, rows, chunk), f32),
            pltpu.VMEM((H, rows, chunk), f32),
            pltpu.VMEM((H, rows, chunk), f32),
            pltpu.VMEM((parts, rows, chunk), f32),
            pltpu.VMEM((H, rows, blk), f32),
            pltpu.VMEM((parts, rows, blk), f32),
            pltpu.VMEM((rows, nodes), f32),
            dma((6,)),
            dma((4,)),
            dma((1,)),
            dma((1,)),
            dma((H,)),
            dma((H,)),
            dma((H,)),
            dma((H,)),
            dma((parts,)),
            dma((parts,)),
            dma((parts,)),
            dma((parts,)),
        ],
        compiler_params=pltpu.CompilerParams(
            collective_id=0, has_side_effects=True, vmem_limit_bytes=63 * 1024 * 1024
        ),
    )(pattern.T, terminals, voltages, conductance, capacitance, samples, forward, backward)


def solution(mesh):
    in_specs = (
        P("harm", "node"),
        P("node", None, None, None),
        P("node", None, None, None),
        P("node", None),
        P(None, "node"),
        P(None, "node"),
    )
    out_specs = P("harm", "node")
    return jax.shard_map(
        per_device, mesh=mesh, in_specs=in_specs, out_specs=out_specs, check_vma=False
    )
```

```python
import functools
import math

import jax
import jax.numpy as jnp
import ml_dtypes
import numpy as np
from jax import lax
from jax.experimental import pallas as pl
from jax.experimental.pallas import tpu as pltpu
from jax.sharding import PartitionSpec as P

MESH = pl.DeviceIdType.MESH
f32, bf16 = jnp.float32, jnp.bfloat16


def halves(value):
    high = value.astype(bf16).astype(f32)
    return jnp.concatenate([high, value - high], axis=0).astype(bf16)


def dot(a, b):
    return jnp.dot(a, b, preferred_element_type=f32)


def dot_t(a, b):
    return lax.dot_general(a, b, (((1,), (1,)), ((), ())), preferred_element_type=f32)


def kernel(
    H, N, parts, dup,
    pat_in, term_in, v_in, g_in, c_in, s_in, f_in, b_in,
    out,
    pat, term, v_vm, g_vm, c_vm, s_vm, f_vm, b_vm,
    vext, halo, ends, send_b, recv_b, send_c, recv_c, send_s, recv_s, lin,
    load_sem, gc_sem,
    low_send, low_recv, halo_send, halo_recv,
    b_send, b_recv, c_send, c_recv, s_send, s_recv,
):
    h, n = lax.axis_index("harm"), lax.axis_index("node")
    rows, nodes = v_vm.shape
    blocks, slots, blk, _ = g_vm.shape
    chunk = s_vm.shape[1]
    part, twin = h // dup, lax.rem(h, dup)
    offset = pl.multiple_of(part * chunk, 128)

    barrier = pltpu.get_barrier_semaphore()

    def greet(to_h, to_n):
        pl.semaphore_signal(barrier, inc=1, device_id=(to_h, to_n), device_id_type=MESH)

    for d in range(1, H):
        greet(lax.rem(h + d, H), n)

    @pl.when(n > 0)
    def _():
        for d in range(H):
            greet(lax.rem(h + d, H), n - 1)

    @pl.when(n < N - 1)
    def _():
        for d in range(H):
            greet(lax.rem(h + d, H), n + 1)

    load_v = pltpu.make_async_copy(v_in, v_vm, load_sem.at[0])
    load_f = pltpu.make_async_copy(f_in, f_vm, load_sem.at[1])
    load_b = pltpu.make_async_copy(b_in, b_vm, load_sem.at[2])
    load_s = pltpu.make_async_copy(s_in.at[:, pl.ds(offset, chunk)], s_vm, load_sem.at[3])
    load_t = pltpu.make_async_copy(term_in, term, load_sem.at[4])
    load_p = pltpu.make_async_copy(pat_in, pat, load_sem.at[5])
    loads = [load_v, load_t, load_p, load_f, load_b, load_s]
    half = blocks // 2
    gc_loads = []
    for k in range(2):
        rng = pl.ds(k * half, half)
        gc_loads.append(pltpu.make_async_copy(g_in.at[rng], g_vm.at[rng], gc_sem.at[2 * k]))
        gc_loads.append(pltpu.make_async_copy(c_in.at[rng], c_vm.at[rng], gc_sem.at[2 * k + 1]))
    for load in loads + gc_loads:
        load.start()

    def greeted():
        sides = jnp.where(n > 0, H, 0) + jnp.where(n < N - 1, H, 0)
        pl.semaphore_wait(barrier, H - 1 + sides)

    def remote(src, dst, send, recv, to_h, to_n):
        return pltpu.make_async_remote_copy(
            src_ref=src, dst_ref=dst, send_sem=send, recv_sem=recv,
            device_id=(to_h, to_n), device_id_type=MESH,
        )

    to_high = remote(
        vext.at[blocks], vext.at[0], low_send.at[0], low_recv.at[0], h, lax.rem(n + 1, N)
    )
    to_low = [
        remote(
            vext.at[1], halo.at[h], halo_send.at[d], halo_recv.at[d],
            lax.rem(h + d, H), lax.rem(n + N - 1, N),
        )
        for d in range(H)
    ]
    spills = []
    for i in range(parts):
        to_h = lax.rem(part + i, parts) * dup + twin
        spills.append(
            remote(send_s.at[to_h], recv_s.at[i], s_send.at[i], s_recv.at[i], to_h, lax.rem(n + 1, N))
        )

    load_t.wait()
    load_v.wait()
    for b in range(blocks):
        vext[b + 1] = v_vm[:, b * blk : (b + 1) * blk]
    stacked = halves(v_vm[...])

    to_parts = []
    step = min(256, nodes)
    for i in [*range(1, parts), 0]:
        q = lax.rem(part + i, parts)
        at = pl.multiple_of(q * chunk, 128)
        first = term[0:1, pl.ds(at, chunk)] - n * nodes
        second = term[1:2, pl.ds(at, chunk)] - n * nodes
        first = jnp.where(first == second, -1, first)
        second = jnp.where(first == -1, -1, second)
        piece = jnp.zeros((2 * rows, chunk), f32)
        for k in range(0, nodes, step):
            row = lax.broadcasted_iota(jnp.int32, (step, chunk), 0) + k
            hot = jnp.where(row == first, 1.0, jnp.where(row == second, -1.0, 0.0)).astype(bf16)
            piece += dot(stacked[:, k : k + step], hot)
        piece = piece[:rows] + piece[rows:]
        if i == 0:
            recv_b[h] = piece
        if i or dup > 1:
            send_b[q] = piece
        if i == (1 if parts > 1 else 0):
            greeted()

            @pl.when(n > 0)
            def _():
                for copy in to_low:
                    copy.start()

            @pl.when(n < N - 1)
            def _():
                to_high.start()

        for j in range(dup):
            if i or j:
                to_h = q * dup + lax.rem(twin + j, dup)
                e = i * dup + j
                copy = remote(send_b.at[q], recv_b.at[h], b_send.at[e], b_recv.at[e], to_h, n)
                copy.start()
                to_parts.append(copy)

    lane = lax.broadcasted_iota(jnp.int32, (chunk, blk), 1)
    for q in range(parts):
        first = term[0:1, q * chunk : (q + 1) * chunk] - n * nodes
        second = term[1:2, q * chunk : (q + 1) * chunk] - n * nodes
        first = jnp.where(first == second, -1, first)
        second = jnp.where(first == -1, -1, second)
        first = jnp.broadcast_to(first, (blk, chunk)).T
        second = jnp.broadcast_to(second, (blk, chunk)).T
        for k in range(0, nodes, blk):
            node = lane + k
            hot = jnp.where(node == first, 1.0, jnp.where(node == second, -1.0, 0.0))
            ends[q, :, k : k + blk] = hot.astype(bf16)

    @pl.when(n > 0)
    def _():
        to_high.wait_recv()

    @pl.when(n == 0)
    def _():
        vext[0] = jnp.zeros((rows, blk), f32)
        recv_s[...] = jnp.zeros(recv_s.shape, f32)

    @pl.when(n < N - 1)
    def _():
        for copy in to_low:
            copy.wait_recv()

    @pl.when(n == N - 1)
    def _():
        halo[...] = jnp.zeros(halo.shape, f32)

    vext[blocks + 1] = halo[h]

    line = lax.broadcasted_iota(jnp.int32, (rows, blk), 0)
    harmonic = h * (rows // 2) + line // 2
    omega = harmonic.astype(f32) / (H * rows // 2)
    odd = lax.rem(line, 2) == 1

    def linear(r):
        at = [jnp.clip(pat[j, r] - (n * blocks - 1), 0, blocks + 1) for j in range(slots)]
        picks = [vext[at[j]] for j in range(slots)]
        picked = halves(jnp.concatenate(picks, axis=1))
        weight = jnp.concatenate(
            [g_vm[r].reshape(slots * blk, blk), c_vm[r].reshape(slots * blk, blk)], axis=1
        )
        high = weight.astype(bf16)
        low = (weight - high.astype(f32)).astype(bf16)
        main = dot(picked, high)
        rest = dot(picked, low)
        both = main[:rows] + (main[rows:] + rest[:rows])
        conductive, capacitive = both[:, :blk], both[:, blk:]
        turned = jnp.where(
            odd, pltpu.roll(capacitive, 1, 0), -pltpu.roll(capacitive, rows - 1, 0)
        )
        lin[:, r * blk : (r + 1) * blk] = conductive + omega * turned

    load_p.wait()

    for copy in to_parts:
        copy.wait_recv()
    first = term[0:1, pl.ds(offset, chunk)] - n * nodes
    second = term[1:2, pl.ds(offset, chunk)] - n * nodes
    row = lax.broadcasted_iota(jnp.int32, (blk, chunk), 0) + nodes
    beyond = jnp.where(row == second, -1.0, 0.0).astype(bf16)
    columns = H * rows
    above = dot(halves(halo[...].reshape(columns, blk)), beyond)
    branch = recv_b[...].reshape(columns, chunk) + (above[:columns] + above[columns:])
    branch_high = branch.astype(bf16)
    branch_low = (branch - branch_high.astype(f32)).astype(bf16)
    load_f.wait()
    load_s.wait()
    wave = dot(f_vm[...], jnp.concatenate([branch_high, branch_low, branch_high], axis=0))
    wave = wave * s_vm[...]
    wave_high = wave.astype(bf16)
    wave_low = (wave - wave_high.astype(f32)).astype(bf16)
    load_b.wait()
    current = dot(b_vm[...], jnp.concatenate([wave_high, wave_low, wave_high], axis=0))
    send_c[...] = current.reshape(H, rows, chunk)
    recv_c[part] = send_c[h]
    to_harm = [None]
    for i in range(1, parts):
        to_h = lax.rem(part + i, parts) * dup + twin
        copy = remote(send_c.at[to_h], recv_c.at[part], c_send.at[i], c_recv.at[i], to_h, n)
        copy.start()
        to_harm.append(copy)
    spill = dot_t(halves(current), beyond)
    send_s[...] = (spill[:columns] + spill[columns:]).reshape(H, rows, blk)

    @pl.when(n < N - 1)
    def _():
        for copy in spills:
            copy.start()

    for load in gc_loads:
        load.wait()
    for r in range(blocks):
        linear(r)

    total = lin[...]
    for i in range(parts):
        q = lax.rem(part + parts - i, parts)
        if i:
            to_harm[i].wait_recv()
        added = dot(halves(recv_c[q]), ends[q])
        total = total + (added[:rows] + added[rows:])

    @pl.when(n > 0)
    def _():
        for copy in spills:
            copy.wait_recv()

    arrival = recv_s[0]
    for i in range(1, parts):
        arrival = arrival + recv_s[i]
    out[:, :blk] = total[:, :blk] + arrival
    out[:, blk:] = total[:, blk:]

    for copy in to_parts + to_harm[1:]:
        copy.wait_send()

    @pl.when(n > 0)
    def _():
        for copy in to_low:
            copy.wait_send()

    @pl.when(n < N - 1)
    def _():
        to_high.wait_send()
        for copy in spills:
            copy.wait_send()


def tables(columns, period):
    harmonic = np.arange(columns // 2)
    phases = (np.arange(period)[:, None] * harmonic[None, :]) % period
    angles = phases * (2.0 * math.pi / period)
    forward = np.stack([np.cos(angles), -np.sin(angles)], axis=2).reshape(period, columns)
    backward = forward.T * (2.0 / period)

    def three(table):
        high = table.astype(ml_dtypes.bfloat16)
        low = (table - high.astype(np.float64)).astype(ml_dtypes.bfloat16)
        return jnp.asarray(np.concatenate([high, high, low], axis=1))

    return three(forward), three(backward)


def per_device(voltages, conductance, capacitance, pattern, samples, terminals):
    rows, nodes = voltages.shape
    blocks, slots, blk, _ = conductance.shape
    period, branches = samples.shape
    H, N = lax.axis_size("harm"), lax.axis_size("node")
    parts = min(H, branches // 128)
    dup = H // parts
    chunk = branches // parts
    forward, backward = tables(H * rows, period)
    dma = pltpu.SemaphoreType.DMA
    anywhere = pl.BlockSpec(memory_space=pltpu.MemorySpace.HBM)
    return pl.pallas_call(
        functools.partial(kernel, H, N, parts, dup),
        out_shape=pltpu.VMEM((rows, nodes), f32),
        in_specs=[anywhere] * 8,
        out_specs=pl.BlockSpec(memory_space=pltpu.MemorySpace.VMEM),
        scratch_shapes=[
            pltpu.SMEM(pattern.shape[::-1], jnp.int32),
            pltpu.VMEM(terminals.shape, jnp.int32),
            pltpu.VMEM((rows, nodes), f32),
            pltpu.VMEM(conductance.shape, f32),
            pltpu.VMEM(capacitance.shape, f32),
            pltpu.VMEM((period, chunk), f32),
            pltpu.VMEM(forward.shape, bf16),
            pltpu.VMEM(backward.shape, bf16),
            pltpu.VMEM((blocks + 2, rows, blk), f32),
            pltpu.VMEM((H, rows, blk), f32),
            pltpu.VMEM((parts, chunk, nodes), bf16),
            pltpu.VMEM((parts, rows, chunk), f32),
            pltpu.VMEM((H, rows, chunk), f32),
            pltpu.VMEM((H, rows, chunk), f32),
            pltpu.VMEM((parts, rows, chunk), f32),
            pltpu.VMEM((H, rows, blk), f32),
            pltpu.VMEM((parts, rows, blk), f32),
            pltpu.VMEM((rows, nodes), f32),
            dma((6,)),
            dma((4,)),
            dma((1,)),
            dma((1,)),
            dma((H,)),
            dma((H,)),
            dma((H,)),
            dma((H,)),
            dma((parts,)),
            dma((parts,)),
            dma((parts,)),
            dma((parts,)),
        ],
        compiler_params=pltpu.CompilerParams(
            collective_id=0, has_side_effects=True, vmem_limit_bytes=63 * 1024 * 1024
        ),
    )(pattern.T, terminals, voltages, conductance, capacitance, samples, forward, backward)


def solution(mesh):
    in_specs = (
        P("harm", "node"),
        P("node", None, None, None),
        P("node", None, None, None),
        P("node", None),
        P(None, "node"),
        P(None, "node"),
    )
    out_specs = P("harm", "node")
    return jax.shard_map(
        per_device, mesh=mesh, in_specs=in_specs, out_specs=out_specs, check_vma=False
    )
```

```python
import functools
import math

import jax
import jax.numpy as jnp
import ml_dtypes
import numpy as np
from jax import lax
from jax.experimental import pallas as pl
from jax.experimental.pallas import tpu as pltpu
from jax.sharding import PartitionSpec as P

MESH = pl.DeviceIdType.MESH
f32, bf16 = jnp.float32, jnp.bfloat16


def halves(value):
    high = value.astype(bf16).astype(f32)
    return jnp.concatenate([high, value - high], axis=0).astype(bf16)


def dot(a, b):
    return jnp.dot(a, b, preferred_element_type=f32)


def kernel(
    H, N, parts, dup,
    pat_in, term_in, v_in, g_in, c_in, s_in, f_in, b_in,
    out,
    pat, term, v_vm, g_vm, c_vm, s_vm, f_vm, b_vm,
    vext, halo, ends, send_b, recv_b, send_c, recv_c, send_s, recv_s, lin,
    load_sem, gc_sem,
    low_send, low_recv, halo_send, halo_recv,
    b_send, b_recv, c_send, c_recv, s_send, s_recv,
):
    h, n = lax.axis_index("harm"), lax.axis_index("node")
    rows, nodes = v_vm.shape
    blocks, slots, blk, _ = g_vm.shape
    chunk = s_vm.shape[1]
    part, twin = h // dup, lax.rem(h, dup)
    offset = pl.multiple_of(part * chunk, 128)

    barrier = pltpu.get_barrier_semaphore()

    def greet(to_h, to_n):
        pl.semaphore_signal(barrier, inc=1, device_id=(to_h, to_n), device_id_type=MESH)

    for d in range(1, H):
        greet(lax.rem(h + d, H), n)

    @pl.when(n > 0)
    def _():
        for d in range(H):
            greet(lax.rem(h + d, H), n - 1)

    @pl.when(n < N - 1)
    def _():
        for d in range(H):
            greet(lax.rem(h + d, H), n + 1)

    load_v = pltpu.make_async_copy(v_in, v_vm, load_sem.at[0])
    load_f = pltpu.make_async_copy(f_in, f_vm, load_sem.at[1])
    load_b = pltpu.make_async_copy(b_in, b_vm, load_sem.at[2])
    load_s = pltpu.make_async_copy(s_in.at[:, pl.ds(offset, chunk)], s_vm, load_sem.at[3])
    load_t = pltpu.make_async_copy(term_in, term, load_sem.at[4])
    load_p = pltpu.make_async_copy(pat_in, pat, load_sem.at[5])
    loads = [load_v, load_t, load_p, load_f, load_b, load_s]
    half = blocks // 2
    gc_loads = []
    for k in range(2):
        rng = pl.ds(k * half, half)
        gc_loads.append(pltpu.make_async_copy(g_in.at[rng], g_vm.at[rng], gc_sem.at[2 * k]))
        gc_loads.append(pltpu.make_async_copy(c_in.at[rng], c_vm.at[rng], gc_sem.at[2 * k + 1]))
    for load in loads + gc_loads:
        load.start()

    def greeted():
        sides = jnp.where(n > 0, H, 0) + jnp.where(n < N - 1, H, 0)
        pl.semaphore_wait(barrier, H - 1 + sides)

    def remote(src, dst, send, recv, to_h, to_n):
        return pltpu.make_async_remote_copy(
            src_ref=src, dst_ref=dst, send_sem=send, recv_sem=recv,
            device_id=(to_h, to_n), device_id_type=MESH,
        )

    to_high = remote(
        vext.at[blocks], vext.at[0], low_send.at[0], low_recv.at[0], h, lax.rem(n + 1, N)
    )
    to_low = [
        remote(
            vext.at[1], halo.at[h], halo_send.at[d], halo_recv.at[d],
            lax.rem(h + d, H), lax.rem(n + N - 1, N),
        )
        for d in range(H)
    ]
    spills = []
    for i in range(parts):
        to_h = lax.rem(part + i, parts) * dup + twin
        spills.append(
            remote(send_s.at[to_h], recv_s.at[i], s_send.at[i], s_recv.at[i], to_h, lax.rem(n + 1, N))
        )

    load_t.wait()
    load_v.wait()
    for b in range(blocks):
        vext[b + 1] = v_vm[:, b * blk : (b + 1) * blk]
    stacked = halves(v_vm[...])

    to_parts = []
    step = min(256, nodes)
    for i in [*range(1, parts), 0]:
        q = lax.rem(part + i, parts)
        at = pl.multiple_of(q * chunk, 128)
        first = term[0:1, pl.ds(at, chunk)] - n * nodes
        second = term[1:2, pl.ds(at, chunk)] - n * nodes
        first = jnp.where(first == second, -1, first)
        second = jnp.where(first == -1, -1, second)
        piece = jnp.zeros((2 * rows, chunk), f32)
        for k in range(0, nodes, step):
            row = lax.broadcasted_iota(jnp.int32, (step, chunk), 0) + k
            hot = jnp.where(row == first, 1.0, jnp.where(row == second, -1.0, 0.0)).astype(bf16)
            piece += dot(stacked[:, k : k + step], hot)
        piece = piece[:rows] + piece[rows:]
        if i == 0:
            recv_b[h] = piece
        if i or dup > 1:
            send_b[q] = piece
        if i == (1 if parts > 1 else 0):
            greeted()

            @pl.when(n > 0)
            def _():
                for copy in to_low:
                    copy.start()

            @pl.when(n < N - 1)
            def _():
                to_high.start()

        for j in range(dup):
            if i or j:
                to_h = q * dup + lax.rem(twin + j, dup)
                e = i * dup + j
                copy = remote(send_b.at[q], recv_b.at[h], b_send.at[e], b_recv.at[e], to_h, n)
                copy.start()
                to_parts.append(copy)

    lane = lax.broadcasted_iota(jnp.int32, (chunk, blk), 1)
    for q in range(parts):
        first = term[0:1, q * chunk : (q + 1) * chunk] - n * nodes
        second = term[1:2, q * chunk : (q + 1) * chunk] - n * nodes
        first = jnp.where(first == second, -1, first)
        second = jnp.where(first == -1, -1, second)
        first = jnp.broadcast_to(first, (blk, chunk)).T
        second = jnp.broadcast_to(second, (blk, chunk)).T
        for k in range(0, nodes, blk):
            node = lane + k
            hot = jnp.where(node == first, 1.0, jnp.where(node == second, -1.0, 0.0))
            ends[q, :, k : k + blk] = hot.astype(bf16)

    @pl.when(n > 0)
    def _():
        to_high.wait_recv()

    @pl.when(n == 0)
    def _():
        vext[0] = jnp.zeros((rows, blk), f32)
        recv_s[...] = jnp.zeros(recv_s.shape, f32)

    @pl.when(n < N - 1)
    def _():
        for copy in to_low:
            copy.wait_recv()

    @pl.when(n == N - 1)
    def _():
        halo[...] = jnp.zeros(halo.shape, f32)

    vext[blocks + 1] = halo[h]

    line = lax.broadcasted_iota(jnp.int32, (rows, blk), 0)
    harmonic = h * (rows // 2) + line // 2
    omega = harmonic.astype(f32) / (H * rows // 2)
    odd = lax.rem(line, 2) == 1

    def linear(r):
        at = [jnp.clip(pat[j, r] - (n * blocks - 1), 0, blocks + 1) for j in range(slots)]
        picks = [vext[at[j]] for j in range(slots)]
        picked = halves(jnp.concatenate(picks, axis=1))
        weight = jnp.concatenate(
            [g_vm[r].reshape(slots * blk, blk), c_vm[r].reshape(slots * blk, blk)], axis=1
        )
        high = weight.astype(bf16)
        low = (weight - high.astype(f32)).astype(bf16)
        main = dot(picked, high)
        rest = dot(picked, low)
        both = main[:rows] + (main[rows:] + rest[:rows])
        conductive, capacitive = both[:, :blk], both[:, blk:]
        turned = jnp.where(
            odd, pltpu.roll(capacitive, 1, 0), -pltpu.roll(capacitive, rows - 1, 0)
        )
        lin[:, r * blk : (r + 1) * blk] = conductive + omega * turned

    load_p.wait()

    first = term[0:1, pl.ds(offset, chunk)] - n * nodes
    second = term[1:2, pl.ds(offset, chunk)] - n * nodes
    row = lax.broadcasted_iota(jnp.int32, (blk, chunk), 0) + nodes
    beyond = jnp.where(row == second, -1.0, 0.0).astype(bf16)
    columns = H * rows
    above = dot(halves(halo[...].reshape(columns, blk)), beyond)
    above = above[:columns] + above[columns:]
    node = lax.broadcasted_iota(jnp.int32, (chunk, blk), 1) + nodes
    second = jnp.broadcast_to(second, (blk, chunk)).T
    beyond_back = jnp.where(node == second, -1.0, 0.0).astype(bf16)
    load_f.wait()
    load_s.wait()
    load_b.wait()
    for copy in to_parts:
        copy.wait_recv()
    branch = recv_b[...].reshape(columns, chunk) + above
    branch_high = branch.astype(bf16)
    branch_low = (branch - branch_high.astype(f32)).astype(bf16)
    wave = dot(f_vm[...], jnp.concatenate([branch_high, branch_low, branch_high], axis=0))
    wave = wave * s_vm[...]
    wave_high = wave.astype(bf16)
    wave_low = (wave - wave_high.astype(f32)).astype(bf16)
    current = dot(b_vm[...], jnp.concatenate([wave_high, wave_low, wave_high], axis=0))
    send_c[...] = current.reshape(H, rows, chunk)
    recv_c[part] = send_c[h]
    to_harm = [None]
    for i in range(1, parts):
        to_h = lax.rem(part + i, parts) * dup + twin
        copy = remote(send_c.at[to_h], recv_c.at[part], c_send.at[i], c_recv.at[i], to_h, n)
        copy.start()
        to_harm.append(copy)
    spill = dot(halves(current), beyond_back)
    send_s[...] = (spill[:columns] + spill[columns:]).reshape(H, rows, blk)

    @pl.when(n < N - 1)
    def _():
        for copy in spills:
            copy.start()

    for load in gc_loads:
        load.wait()
    for r in range(blocks):
        linear(r)

    total = lin[...]
    for i in range(parts):
        q = lax.rem(part + parts - i, parts)
        if i:
            to_harm[i].wait_recv()
        added = dot(halves(recv_c[q]), ends[q])
        total = total + (added[:rows] + added[rows:])

    @pl.when(n > 0)
    def _():
        for copy in spills:
            copy.wait_recv()

    arrival = recv_s[0]
    for i in range(1, parts):
        arrival = arrival + recv_s[i]
    out[:, :blk] = total[:, :blk] + arrival
    out[:, blk:] = total[:, blk:]

    for copy in to_parts + to_harm[1:]:
        copy.wait_send()

    @pl.when(n > 0)
    def _():
        for copy in to_low:
            copy.wait_send()

    @pl.when(n < N - 1)
    def _():
        to_high.wait_send()
        for copy in spills:
            copy.wait_send()


def tables(columns, period):
    harmonic = np.arange(columns // 2)
    phases = (np.arange(period)[:, None] * harmonic[None, :]) % period
    angles = phases * (2.0 * math.pi / period)
    forward = np.stack([np.cos(angles), -np.sin(angles)], axis=2).reshape(period, columns)
    backward = forward.T * (2.0 / period)

    def three(table):
        high = table.astype(ml_dtypes.bfloat16)
        low = (table - high.astype(np.float64)).astype(ml_dtypes.bfloat16)
        return jnp.asarray(np.concatenate([high, high, low], axis=1))

    return three(forward), three(backward)


def per_device(voltages, conductance, capacitance, pattern, samples, terminals):
    rows, nodes = voltages.shape
    blocks, slots, blk, _ = conductance.shape
    period, branches = samples.shape
    H, N = lax.axis_size("harm"), lax.axis_size("node")
    parts = min(H, branches // 128)
    dup = H // parts
    chunk = branches // parts
    forward, backward = tables(H * rows, period)
    dma = pltpu.SemaphoreType.DMA
    anywhere = pl.BlockSpec(memory_space=pltpu.MemorySpace.HBM)
    return pl.pallas_call(
        functools.partial(kernel, H, N, parts, dup),
        out_shape=pltpu.VMEM((rows, nodes), f32),
        in_specs=[anywhere] * 8,
        out_specs=pl.BlockSpec(memory_space=pltpu.MemorySpace.VMEM),
        scratch_shapes=[
            pltpu.SMEM(pattern.shape[::-1], jnp.int32),
            pltpu.VMEM(terminals.shape, jnp.int32),
            pltpu.VMEM((rows, nodes), f32),
            pltpu.VMEM(conductance.shape, f32),
            pltpu.VMEM(capacitance.shape, f32),
            pltpu.VMEM((period, chunk), f32),
            pltpu.VMEM(forward.shape, bf16),
            pltpu.VMEM(backward.shape, bf16),
            pltpu.VMEM((blocks + 2, rows, blk), f32),
            pltpu.VMEM((H, rows, blk), f32),
            pltpu.VMEM((parts, chunk, nodes), bf16),
            pltpu.VMEM((parts, rows, chunk), f32),
            pltpu.VMEM((H, rows, chunk), f32),
            pltpu.VMEM((H, rows, chunk), f32),
            pltpu.VMEM((parts, rows, chunk), f32),
            pltpu.VMEM((H, rows, blk), f32),
            pltpu.VMEM((parts, rows, blk), f32),
            pltpu.VMEM((rows, nodes), f32),
            dma((6,)),
            dma((4,)),
            dma((1,)),
            dma((1,)),
            dma((H,)),
            dma((H,)),
            dma((H,)),
            dma((H,)),
            dma((parts,)),
            dma((parts,)),
            dma((parts,)),
            dma((parts,)),
        ],
        compiler_params=pltpu.CompilerParams(
            collective_id=0, has_side_effects=True, vmem_limit_bytes=63 * 1024 * 1024
        ),
    )(pattern.T, terminals, voltages, conductance, capacitance, samples, forward, backward)


def solution(mesh):
    in_specs = (
        P("harm", "node"),
        P("node", None, None, None),
        P("node", None, None, None),
        P("node", None),
        P(None, "node"),
        P(None, "node"),
    )
    out_specs = P("harm", "node")
    return jax.shard_map(
        per_device, mesh=mesh, in_specs=in_specs, out_specs=out_specs, check_vma=False
    )
```

```python
import functools
import math

import jax
import jax.numpy as jnp
import ml_dtypes
import numpy as np
from jax import lax
from jax.experimental import pallas as pl
from jax.experimental.pallas import tpu as pltpu
from jax.sharding import PartitionSpec as P

MESH = pl.DeviceIdType.MESH
f32, bf16 = jnp.float32, jnp.bfloat16


def halves(value):
    high = value.astype(bf16).astype(f32)
    return jnp.concatenate([high, value - high], axis=0).astype(bf16)


def dot(a, b):
    return jnp.dot(a, b, preferred_element_type=f32)


def kernel(
    H, N, parts, dup,
    pat_in, term_in, v_in, g_in, c_in, s_in, f_in, b_in,
    out,
    pat, term, v_vm, g_vm, c_vm, s_vm, f_vm, b_vm,
    vext, halo, ends, send_b, recv_b, send_c, recv_c, send_s, recv_s, lin,
    load_sem, gc_sem,
    low_send, low_recv, halo_send, halo_recv,
    b_send, b_recv, c_send, c_recv, s_send, s_recv,
):
    h, n = lax.axis_index("harm"), lax.axis_index("node")
    rows, nodes = v_vm.shape
    blocks, slots, blk, _ = g_vm.shape
    chunk = s_vm.shape[1]
    part, twin = h // dup, lax.rem(h, dup)
    offset = pl.multiple_of(part * chunk, 128)

    barrier = pltpu.get_barrier_semaphore()

    def greet(to_h, to_n):
        pl.semaphore_signal(barrier, inc=1, device_id=(to_h, to_n), device_id_type=MESH)

    for d in range(1, H):
        greet(lax.rem(h + d, H), n)

    @pl.when(n > 0)
    def _():
        for d in range(H):
            greet(lax.rem(h + d, H), n - 1)

    @pl.when(n < N - 1)
    def _():
        for d in range(H):
            greet(lax.rem(h + d, H), n + 1)

    load_v = pltpu.make_async_copy(v_in, v_vm, load_sem.at[0])
    load_f = pltpu.make_async_copy(f_in, f_vm, load_sem.at[1])
    load_b = pltpu.make_async_copy(b_in, b_vm, load_sem.at[2])
    load_s = pltpu.make_async_copy(s_in.at[:, pl.ds(offset, chunk)], s_vm, load_sem.at[3])
    load_t = pltpu.make_async_copy(term_in, term, load_sem.at[4])
    load_p = pltpu.make_async_copy(pat_in, pat, load_sem.at[5])
    loads = [load_v, load_t, load_p, load_f, load_b, load_s]
    half = blocks // 2
    gc_loads = []
    for k in range(2):
        rng = pl.ds(k * half, half)
        gc_loads.append(pltpu.make_async_copy(g_in.at[rng], g_vm.at[rng], gc_sem.at[2 * k]))
        gc_loads.append(pltpu.make_async_copy(c_in.at[rng], c_vm.at[rng], gc_sem.at[2 * k + 1]))
    for load in loads:
        load.start()

    def greeted():
        sides = jnp.where(n > 0, H, 0) + jnp.where(n < N - 1, H, 0)
        pl.semaphore_wait(barrier, H - 1 + sides)

    def remote(src, dst, send, recv, to_h, to_n):
        return pltpu.make_async_remote_copy(
            src_ref=src, dst_ref=dst, send_sem=send, recv_sem=recv,
            device_id=(to_h, to_n), device_id_type=MESH,
        )

    to_high = remote(
        vext.at[blocks], vext.at[0], low_send.at[0], low_recv.at[0], h, lax.rem(n + 1, N)
    )
    to_low = [
        remote(
            vext.at[1], halo.at[h], halo_send.at[d], halo_recv.at[d],
            lax.rem(h + d, H), lax.rem(n + N - 1, N),
        )
        for d in range(H)
    ]
    spills = []
    for i in range(parts):
        to_h = lax.rem(part + i, parts) * dup + twin
        spills.append(
            remote(send_s.at[to_h], recv_s.at[i], s_send.at[i], s_recv.at[i], to_h, lax.rem(n + 1, N))
        )

    load_t.wait()
    load_v.wait()
    for load in gc_loads:
        load.start()
    for b in range(blocks):
        vext[b + 1] = v_vm[:, b * blk : (b + 1) * blk]
    stacked = halves(v_vm[...])

    to_parts = []
    step = min(256, nodes)
    for i in [*range(1, parts), 0]:
        q = lax.rem(part + i, parts)
        at = pl.multiple_of(q * chunk, 128)
        first = term[0:1, pl.ds(at, chunk)] - n * nodes
        second = term[1:2, pl.ds(at, chunk)] - n * nodes
        first = jnp.where(first == second, -1, first)
        second = jnp.where(first == -1, -1, second)
        piece = jnp.zeros((2 * rows, chunk), f32)
        for k in range(0, nodes, step):
            row = lax.broadcasted_iota(jnp.int32, (step, chunk), 0) + k
            hot = jnp.where(row == first, 1.0, jnp.where(row == second, -1.0, 0.0)).astype(bf16)
            piece += dot(stacked[:, k : k + step], hot)
        piece = piece[:rows] + piece[rows:]
        if i == 0:
            recv_b[h] = piece
        if i or dup > 1:
            send_b[q] = piece
        if i == (1 if parts > 1 else 0):
            greeted()

            @pl.when(n > 0)
            def _():
                for copy in to_low:
                    copy.start()

            @pl.when(n < N - 1)
            def _():
                to_high.start()

        for j in range(dup):
            if i or j:
                to_h = q * dup + lax.rem(twin + j, dup)
                e = i * dup + j
                copy = remote(send_b.at[q], recv_b.at[h], b_send.at[e], b_recv.at[e], to_h, n)
                copy.start()
                to_parts.append(copy)

    lane = lax.broadcasted_iota(jnp.int32, (chunk, blk), 1)
    for q in range(parts):
        first = term[0:1, q * chunk : (q + 1) * chunk] - n * nodes
        second = term[1:2, q * chunk : (q + 1) * chunk] - n * nodes
        first = jnp.where(first == second, -1, first)
        second = jnp.where(first == -1, -1, second)
        first = jnp.broadcast_to(first, (blk, chunk)).T
        second = jnp.broadcast_to(second, (blk, chunk)).T
        for k in range(0, nodes, blk):
            node = lane + k
            hot = jnp.where(node == first, 1.0, jnp.where(node == second, -1.0, 0.0))
            ends[q, :, k : k + blk] = hot.astype(bf16)

    @pl.when(n > 0)
    def _():
        to_high.wait_recv()

    @pl.when(n == 0)
    def _():
        vext[0] = jnp.zeros((rows, blk), f32)
        recv_s[...] = jnp.zeros(recv_s.shape, f32)

    @pl.when(n < N - 1)
    def _():
        for copy in to_low:
            copy.wait_recv()

    @pl.when(n == N - 1)
    def _():
        halo[...] = jnp.zeros(halo.shape, f32)

    vext[blocks + 1] = halo[h]

    line = lax.broadcasted_iota(jnp.int32, (rows, blk), 0)
    harmonic = h * (rows // 2) + line // 2
    omega = harmonic.astype(f32) / (H * rows // 2)
    odd = lax.rem(line, 2) == 1

    def linear(r):
        at = [jnp.clip(pat[j, r] - (n * blocks - 1), 0, blocks + 1) for j in range(slots)]
        picks = [vext[at[j]] for j in range(slots)]
        picked = halves(jnp.concatenate(picks, axis=1))
        weight = jnp.concatenate(
            [g_vm[r].reshape(slots * blk, blk), c_vm[r].reshape(slots * blk, blk)], axis=1
        )
        high = weight.astype(bf16)
        low = (weight - high.astype(f32)).astype(bf16)
        main = dot(picked, high)
        rest = dot(picked, low)
        both = main[:rows] + (main[rows:] + rest[:rows])
        conductive, capacitive = both[:, :blk], both[:, blk:]
        turned = jnp.where(
            odd, pltpu.roll(capacitive, 1, 0), -pltpu.roll(capacitive, rows - 1, 0)
        )
        lin[:, r * blk : (r + 1) * blk] = conductive + omega * turned

    load_p.wait()

    first = term[0:1, pl.ds(offset, chunk)] - n * nodes
    second = term[1:2, pl.ds(offset, chunk)] - n * nodes
    row = lax.broadcasted_iota(jnp.int32, (blk, chunk), 0) + nodes
    beyond = jnp.where(row == second, -1.0, 0.0).astype(bf16)
    columns = H * rows
    above = dot(halves(halo[...].reshape(columns, blk)), beyond)
    above = above[:columns] + above[columns:]
    node = lax.broadcasted_iota(jnp.int32, (chunk, blk), 1) + nodes
    second = jnp.broadcast_to(second, (blk, chunk)).T
    beyond_back = jnp.where(node == second, -1.0, 0.0).astype(bf16)
    load_f.wait()
    load_s.wait()
    load_b.wait()
    for copy in to_parts:
        copy.wait_recv()
    branch = recv_b[...].reshape(columns, chunk) + above
    branch_high = branch.astype(bf16)
    branch_low = (branch - branch_high.astype(f32)).astype(bf16)
    wave = dot(f_vm[...], jnp.concatenate([branch_high, branch_low, branch_high], axis=0))
    wave = wave * s_vm[...]
    wave_high = wave.astype(bf16)
    wave_low = (wave - wave_high.astype(f32)).astype(bf16)
    current = dot(b_vm[...], jnp.concatenate([wave_high, wave_low, wave_high], axis=0))
    send_c[...] = current.reshape(H, rows, chunk)
    recv_c[part] = send_c[h]
    to_harm = [None]
    for i in range(1, parts):
        to_h = lax.rem(part + i, parts) * dup + twin
        copy = remote(send_c.at[to_h], recv_c.at[part], c_send.at[i], c_recv.at[i], to_h, n)
        copy.start()
        to_harm.append(copy)
    spill = dot(halves(current), beyond_back)
    send_s[...] = (spill[:columns] + spill[columns:]).reshape(H, rows, blk)

    @pl.when(n < N - 1)
    def _():
        for copy in spills:
            copy.start()

    for load in gc_loads:
        load.wait()
    for r in range(blocks):
        linear(r)

    total = lin[...]
    for i in range(parts):
        q = lax.rem(part + parts - i, parts)
        if i:
            to_harm[i].wait_recv()
        added = dot(halves(recv_c[q]), ends[q])
        total = total + (added[:rows] + added[rows:])

    @pl.when(n > 0)
    def _():
        for copy in spills:
            copy.wait_recv()

    arrival = recv_s[0]
    for i in range(1, parts):
        arrival = arrival + recv_s[i]
    out[:, :blk] = total[:, :blk] + arrival
    out[:, blk:] = total[:, blk:]

    for copy in to_parts + to_harm[1:]:
        copy.wait_send()

    @pl.when(n > 0)
    def _():
        for copy in to_low:
            copy.wait_send()

    @pl.when(n < N - 1)
    def _():
        to_high.wait_send()
        for copy in spills:
            copy.wait_send()


def tables(columns, period):
    harmonic = np.arange(columns // 2)
    phases = (np.arange(period)[:, None] * harmonic[None, :]) % period
    angles = phases * (2.0 * math.pi / period)
    forward = np.stack([np.cos(angles), -np.sin(angles)], axis=2).reshape(period, columns)
    backward = forward.T * (2.0 / period)

    def three(table):
        high = table.astype(ml_dtypes.bfloat16)
        low = (table - high.astype(np.float64)).astype(ml_dtypes.bfloat16)
        return jnp.asarray(np.concatenate([high, high, low], axis=1))

    return three(forward), three(backward)


def per_device(voltages, conductance, capacitance, pattern, samples, terminals):
    rows, nodes = voltages.shape
    blocks, slots, blk, _ = conductance.shape
    period, branches = samples.shape
    H, N = lax.axis_size("harm"), lax.axis_size("node")
    parts = min(H, branches // 128)
    dup = H // parts
    chunk = branches // parts
    forward, backward = tables(H * rows, period)
    dma = pltpu.SemaphoreType.DMA
    anywhere = pl.BlockSpec(memory_space=pltpu.MemorySpace.HBM)
    return pl.pallas_call(
        functools.partial(kernel, H, N, parts, dup),
        out_shape=pltpu.VMEM((rows, nodes), f32),
        in_specs=[anywhere] * 8,
        out_specs=pl.BlockSpec(memory_space=pltpu.MemorySpace.VMEM),
        scratch_shapes=[
            pltpu.SMEM(pattern.shape[::-1], jnp.int32),
            pltpu.VMEM(terminals.shape, jnp.int32),
            pltpu.VMEM((rows, nodes), f32),
            pltpu.VMEM(conductance.shape, f32),
            pltpu.VMEM(capacitance.shape, f32),
            pltpu.VMEM((period, chunk), f32),
            pltpu.VMEM(forward.shape, bf16),
            pltpu.VMEM(backward.shape, bf16),
            pltpu.VMEM((blocks + 2, rows, blk), f32),
            pltpu.VMEM((H, rows, blk), f32),
            pltpu.VMEM((parts, chunk, nodes), bf16),
            pltpu.VMEM((parts, rows, chunk), f32),
            pltpu.VMEM((H, rows, chunk), f32),
            pltpu.VMEM((H, rows, chunk), f32),
            pltpu.VMEM((parts, rows, chunk), f32),
            pltpu.VMEM((H, rows, blk), f32),
            pltpu.VMEM((parts, rows, blk), f32),
            pltpu.VMEM((rows, nodes), f32),
            dma((6,)),
            dma((4,)),
            dma((1,)),
            dma((1,)),
            dma((H,)),
            dma((H,)),
            dma((H,)),
            dma((H,)),
            dma((parts,)),
            dma((parts,)),
            dma((parts,)),
            dma((parts,)),
        ],
        compiler_params=pltpu.CompilerParams(
            collective_id=0, has_side_effects=True, vmem_limit_bytes=63 * 1024 * 1024
        ),
    )(pattern.T, terminals, voltages, conductance, capacitance, samples, forward, backward)


def solution(mesh):
    in_specs = (
        P("harm", "node"),
        P("node", None, None, None),
        P("node", None, None, None),
        P("node", None),
        P(None, "node"),
        P(None, "node"),
    )
    out_specs = P("harm", "node")
    return jax.shard_map(
        per_device, mesh=mesh, in_specs=in_specs, out_specs=out_specs, check_vma=False
    )
```
